32 devices in a mesh: dp: 2 (over y), expert: 16 (over z, x, core).
Axes of the slice: x: 2, y: 2, z: 4, core: 2. Of those that a mesh axis runs over, the one named last changes fastest.
Arguments:
- hidden_states: bfloat16 [256, 4, 4096], P('expert'), may hold values from -6 to 6
- routes: int32 [256, 4, 8], P('expert'), may hold values from 0 to 15, all different within a row; in each aligned block of 64 rows (0 to 63, 64 to 127, ..., all dimensions but the last counted through in order) at most 64 rows name the same one
- route_weight: float32 [256, 4, 8], P('expert'), may hold values from 0.05 to 1
- finish_step: int32 [256], P('expert'), may hold values from 1 to 4
- group_keep: int32 [16], P('expert'), may hold values from 0 to 1
- dest_slot: int32 [256], P('expert'), may hold values from 0 to 255, as said below
- w_gate: bfloat16 [16, 4096, 1536], P('expert', None, 'dp'), may hold values from -0.09375 to 0.09375
- w_up: bfloat16 [16, 4096, 1536], P('expert', None, 'dp'), may hold values from -0.09375 to 0.09375
- w_down: bfloat16 [16, 1536, 4096], P('expert', 'dp'), may hold values from -0.15625 to 0.15625
Outputs:
- trainer_rows: bfloat16 [256, 4, 4096], P(('dp', 'expert'))
The draws below stay inside these ranges and needn't reach their ends.
Inputs may be any that keep to these rules, and one draw needn't show every extreme that they name: `routes`: in the 64 row-steps of one prompt group (rows g * 16 to (g + 1) * 16 - 1, all steps), no expert is named more than 64 times, a bound that some block reaches; a row names 8 different experts at each step. dest_slot is a permutation of the slots; row r of group g = r // 16 goes to a slot (d * 16 + g) * 8 + i with 0 <= d < 2 and 0 <= i < 8.
All inputs are finite; a program needn't handle non-finite values.
Results may differ from the reference program's by a relative error of at most 0.0049.
Values may be sent and summed in bfloat16 or wider, within the bound.
A program may use at most 128 MiB of HBM per device.

```python
import math
import jax
import jax.numpy as jnp
import numpy as np
from jax import lax

D = 4096
FF = 1536
TOP = 8
STEPS = 4
ROW_DEV = 16
EXPERTS = 16
ROWS = 256
MOST = 64
SHARE = 8


def draw_dest_slot(key, part):
    group_total = ROWS // ROW_DEV
    group_keys = jax.random.split(jax.random.fold_in(key, 7), group_total)
    shuffled = jax.vmap(lambda one_key: jax.random.permutation(one_key, ROW_DEV))(group_keys)
    replica_of = shuffled // SHARE
    within = shuffled % SHARE
    group_index = jnp.arange(group_total, dtype=jnp.int32)[:, None]
    slots_out = (replica_of * group_total + group_index) * SHARE + within
    return slots_out.reshape(-1).astype(jnp.int32)


def draw_finish_step(key, part):
    first_key, second_key = jax.random.split(jax.random.fold_in(key, 11))
    codes = jax.random.randint(first_key, (ROWS,), 0, 20)
    table = jnp.array([4] * 16 + [1, 2, 3, 3], dtype=jnp.int32)
    values = table[codes]
    order = jax.random.permutation(second_key, ROWS)
    values = values.at[order[0]].set(1).at[order[1]].set(STEPS)
    return values.astype(jnp.int32)


def draw_group_keep(key, part):
    first_key, second_key = jax.random.split(jax.random.fold_in(key, 13))
    codes = jax.random.randint(first_key, (EXPERTS,), 0, 8)
    values = jnp.where(codes == 0, 0, 1).astype(jnp.int32)
    order = jax.random.permutation(second_key, EXPERTS)
    values = values.at[order[0]].set(0).at[order[1]].set(1)
    return values.astype(jnp.int32)


def steps_of(own_key, shape, shards, smallest, largest):
    def one(dim, shards_of):
        steps = jax.random.uniform(jax.random.fold_in(jax.random.fold_in(own_key, 6), dim), (shards_of,), jnp.float32, smallest / len(shards), largest / len(shards))
        return jnp.repeat(jnp.exp(steps), shape[dim] // shards_of).reshape((-1,) + (1,) * (len(shape) - dim - 1))

    level = one(*shards[0])
    for cut in shards[1:]:
        level = level * one(*cut)
    return level


def assign_block(own_key, own, number, rows, number_of, top, limit, lean):
    sequence = jax.random.permutation(own_key, number_of)
    packed, ordinary = portions_of(number_of, rows * top, limit, lean, True), portions_of(number_of, rows * top, limit, lean, False)
    places = jnp.arange(number_of)

    def named(sizes, turn):
        used = int((sizes > 0).sum())
        fixed = max(1, used // 4)
        passed = fixed + (places - fixed + turn * (used - fixed)) % max(1, number_of - fixed)
        return jnp.zeros((number_of,), jnp.int32).at[sequence[jnp.where(places < fixed, places, passed)]].set(jnp.asarray(sizes, jnp.int32))

    sizes = jnp.where(number % 4 == 0, named(packed, number // 4), named(ordinary, number - number // 4 - 1))
    mixed = jax.random.permutation(jax.random.fold_in(own, 3), number_of)
    source_of, receiver = mixed[0:number_of // 2 * 2:2], mixed[1:number_of // 2 * 2:2]
    room = jnp.minimum(sizes[source_of] - 1, limit - sizes[receiver]) // 2
    room = jnp.where((source_of == sequence[0]) | (receiver == sequence[0]) | (sizes[receiver] == 0), 0, jnp.maximum(room, 0))
    passed = jax.random.randint(jax.random.fold_in(own, 4), (number_of // 2,), 0, 1 << 20) % (room + 1)
    sizes = sizes.at[source_of].add(-passed).at[receiver].add(passed)
    labels = jnp.searchsorted(jnp.cumsum(sizes), jnp.arange(rows * top), side="right").astype(jnp.int32)
    table = labels.reshape(top, rows).T
    table = table[jax.random.permutation(jax.random.fold_in(own, 1), rows)]
    turn = jax.random.randint(jax.random.fold_in(own, 2), (rows, 1), 0, top)
    return jnp.take_along_axis(table, (jnp.arange(top)[None, :] + turn) % top, axis=1)


def portions_of(amount, total, reach, skew, full):
    portions = [(1 << 20) // math.isqrt(standing ** skew) + 1 for standing in range(1, amount + 1)]
    largest = reach if full else min(reach, max(-(-total // amount), total * portions[0] // sum(portions)))
    least = 1 if total - largest >= amount - 1 else 0
    given, rest = [largest] + [least] * (amount - 1), total - largest - least * (amount - 1)
    while rest > 0:
        movable = [i for i in range(1, amount) if given[i] < largest] or [i for i in range(1, amount) if given[i] < reach]
        mass, left = sum([portions[i] for i in movable]), rest
        for i in movable:
            addition = min(reach - given[i], max(1, left * portions[i] // mass), rest)
            given[i] = given[i] + addition
            rest = rest - addition
    return np.array(given)


def gaussian(key, extent, width, reach, shards=(), held_as=jnp.bfloat16):
    entries = jax.random.normal(key, extent, jnp.float32) * width
    if len(shards) > 0:
        entries = steps_of(key, extent, shards, -0.22, 0.18) * entries
    return jnp.clip(entries, min=-reach, max=reach).astype(held_as)


def setup_inputs(seed: int = 0) -> dict:
    splits = jax.random.split(jax.random.key(seed), 10)
    hidden_states = gaussian(splits[0], (ROWS, STEPS, D), 1.0, 6.0, ((0, 16),))
    routes_keys = jax.random.split(jax.random.fold_in(splits[1], 1), ROWS * STEPS // (ROW_DEV * STEPS))
    routes_turns = jax.random.permutation(jax.random.fold_in(splits[1], 3), ROWS * STEPS // (ROW_DEV * STEPS))
    routes = jax.vmap(lambda own, number: assign_block(jax.random.fold_in(splits[1], 2), own, number, ROW_DEV * STEPS, EXPERTS, TOP, MOST, 2))(routes_keys, routes_turns).reshape((ROWS, STEPS, TOP))
    route_weight = jnp.clip(jnp.exp(math.log(1.0) - 2.9957323 * jax.random.uniform(splits[2], (ROWS, STEPS, TOP), jnp.float32) ** steps_of(splits[2], (ROWS, STEPS, TOP), ((0, 16),), -0.2, 0.2)), 0.05, 1.0)
    finish_step = draw_finish_step(jax.random.fold_in(splits[9], 71), 0)
    group_keep = draw_group_keep(jax.random.fold_in(splits[9], 71), 0)
    dest_slot = draw_dest_slot(jax.random.fold_in(splits[9], 71), 0)
    w_gate = gaussian(splits[6], (EXPERTS, D, FF), D ** -0.5, 0.09375, ((0, 16), (2, 2)))
    w_up = gaussian(splits[7], (EXPERTS, D, FF), D ** -0.5, 0.09375, ((0, 16), (2, 2)))
    w_down = gaussian(splits[8], (EXPERTS, FF, D), FF ** -0.5, 0.15625, ((0, 16), (1, 2)))
    return dict(hidden_states=hidden_states, routes=routes, route_weight=route_weight, finish_step=finish_step, group_keep=group_keep, dest_slot=dest_slot, w_gate=w_gate, w_up=w_up, w_down=w_down)


def reference(hidden_states, routes, route_weight, finish_step, group_keep, dest_slot, w_gate, w_up, w_down):
    tokens = ROWS * STEPS
    capacity = MOST * (ROWS // ROW_DEV)
    step_ids = jnp.arange(STEPS, dtype=jnp.int32)
    keep_rows = jnp.repeat(group_keep, ROW_DEV)
    live_mask = ((step_ids[None, :] < finish_step[:, None]) & (keep_rows[:, None] == 1)).reshape(tokens)
    gate_share = route_weight / jnp.sum(route_weight, axis=2, keepdims=True)
    flat_inputs = hidden_states.reshape(tokens, D)
    flat_routes = routes.reshape(tokens, TOP)
    flat_share = gate_share.reshape(tokens, TOP)

    def per_expert(running, expert):
        picked = (flat_routes == expert) & live_mask[:, None]
        weight = jnp.sum(jnp.where(picked, flat_share, jnp.zeros_like(flat_share)), axis=1)
        hit_mask = jnp.any(picked, axis=1)
        picked_rows = jnp.nonzero(hit_mask, size=capacity, fill_value=0)[0].astype(jnp.int32)
        filled = jnp.arange(capacity, dtype=jnp.int32) < jnp.sum(hit_mask.astype(jnp.int32))
        rows_in = flat_inputs[picked_rows].astype(jnp.float32)
        gate_part = jnp.dot(rows_in, w_gate[expert].astype(jnp.float32), precision=lax.Precision.HIGHEST)
        up_part = jnp.dot(rows_in, w_up[expert].astype(jnp.float32), precision=lax.Precision.HIGHEST)
        activated = (jax.nn.silu(gate_part) * up_part).astype(jnp.bfloat16)
        expert_result = jnp.dot(activated.astype(jnp.float32), w_down[expert].astype(jnp.float32), precision=lax.Precision.HIGHEST)
        scale = jnp.where(filled, weight[picked_rows], jnp.zeros_like(weight[picked_rows]))
        running = running.at[picked_rows].add(scale[:, None] * expert_result)
        return running, None

    start = jnp.zeros((tokens, D), jnp.float32)
    combined, _ = lax.scan(per_expert, start, jnp.arange(EXPERTS, dtype=jnp.int32))
    combined = combined.reshape(ROWS, STEPS, D).astype(jnp.bfloat16)
    trainer_rows = jnp.zeros((ROWS, STEPS, D), jnp.bfloat16).at[dest_slot].set(combined)
    return trainer_rows
```

```python
import jax
import jax.numpy as jnp
from jax import lax
from jax.sharding import PartitionSpec as P

CHUNKS = 2


def to_send(kept):
    return kept.astype(jnp.bfloat16)


def fold_bit(value, dim, bit, axis, pairs):
    low = lax.index_in_dim(value, 0, dim, keepdims=False)
    high = lax.index_in_dim(value, 1, dim, keepdims=False)
    kept = jnp.where(bit == 0, low, high)
    sent = jnp.where(bit == 0, high, low)
    arrived = lax.ppermute(sent, axis, pairs)
    return to_send(kept.astype(jnp.float32) + arrived.astype(jnp.float32))


def fold_many(value, count, me, axis, pairs_of):
    total = lax.dynamic_index_in_dim(value, me, 0, keepdims=False).astype(jnp.float32)
    for shift in range(1, count):
        block = lax.dynamic_index_in_dim(value, (me + shift) % count, 0, keepdims=False)
        total = total + lax.ppermute(block, axis, pairs_of(shift)).astype(jnp.float32)
    return to_send(total)


def body(
    hidden_states, routes, route_weight, finish_step, group_keep, dest_slot, w_gate, w_up, w_down
):
    expert_count = lax.axis_size("expert")
    replica_count = lax.axis_size("dp")
    row_count, step_count, model_width = hidden_states.shape
    share_rows = row_count // replica_count
    place = dest_slot // (share_rows * expert_count) * share_rows + dest_slot % share_rows
    order = place[None, :] == lax.broadcasted_iota(jnp.int32, (row_count, row_count), 0)
    step_ids = lax.broadcasted_iota(jnp.int32, (row_count, step_count), 1)
    live = (step_ids < finish_step[:, None]) & (group_keep[0] == 1)
    gate_share = route_weight / jnp.sum(route_weight, axis=2, keepdims=True)
    expert_ids = lax.broadcasted_iota(jnp.int32, (1, 1, 1, expert_count), 3)
    picked = (routes[..., None] == expert_ids) & live[:, :, None, None]
    weight = jnp.sum(jnp.where(picked, gate_share[..., None], 0.0), axis=2)
    weight = jnp.sum(jnp.where(order[:, :, None, None], weight[None], 0.0), axis=1)
    my_expert = lax.axis_index("expert")
    my_replica = lax.axis_index("dp")
    all_weight = lax.all_gather(weight, "expert", axis=0, tiled=False)
    mine = lax.broadcasted_iota(jnp.int32, all_weight.shape, 3) == my_expert
    my_weight = jnp.sum(jnp.where(mine, all_weight, 0.0), axis=3)
    ordered = jnp.dot(
        order.astype(jnp.bfloat16),
        hidden_states.reshape(row_count, step_count * model_width),
        preferred_element_type=jnp.float32,
    ).astype(jnp.bfloat16).reshape(row_count, step_count, model_width)
    part = step_count // CHUNKS
    quad_count = expert_count // 4
    core_bit, side_bit, quad = my_expert % 2, my_expert // 2 % 2, my_expert // 4
    core_pairs = [(e, e ^ 1) for e in range(expert_count)]
    side_pairs = [(e, e ^ 2) for e in range(expert_count)]

    def quad_pairs(shift):
        return [(e, (e + 4 * shift) % expert_count) for e in range(expert_count)]

    def replica_pairs(shift):
        return [(d, (d + shift) % replica_count) for d in range(replica_count)]

    results = []
    for c in range(CHUNKS):
        steps = slice(c * part, (c + 1) * part)
        rows = ordered[:, steps].reshape(replica_count * share_rows * part, model_width)
        gathered = lax.all_gather(rows, "expert", axis=0, tiled=True)
        gate_part = jnp.dot(gathered, w_gate[0], preferred_element_type=jnp.float32)
        up_part = jnp.dot(gathered, w_up[0], preferred_element_type=jnp.float32)
        activated = (jax.nn.silu(gate_part) * up_part).astype(jnp.bfloat16)
        expert_result = jnp.dot(activated, w_down[0], preferred_element_type=jnp.float32)
        scale = my_weight[:, :, steps].reshape(-1, 1)
        partial_out = to_send(expert_result * scale)
        held = partial_out.reshape(
            quad_count, 2, 2, replica_count, share_rows * part, model_width
        )
        held = fold_bit(held, 2, core_bit, "expert", core_pairs)
        half = model_width // 2
        first, second = held[..., :half], held[..., half:]
        first = fold_bit(first, 1, side_bit, "expert", side_pairs)
        first = fold_many(first.swapaxes(0, 1), replica_count, my_replica, "dp", replica_pairs)
        second = fold_many(
            second.transpose(2, 0, 1, 3, 4), replica_count, my_replica, "dp", replica_pairs
        )
        second = fold_bit(second, 1, side_bit, "expert", side_pairs)
        first = fold_many(first, quad_count, quad, "expert", quad_pairs)
        second = fold_many(second, quad_count, quad, "expert", quad_pairs)
        summed = jnp.concatenate([first, second], axis=-1)
        results.append(summed.reshape(share_rows, part, model_width))
    return jnp.concatenate(results, axis=1)


def solution(mesh):
    in_specs = (
        P("expert", None, None),
        P("expert", None, None),
        P("expert", None, None),
        P("expert"),
        P("expert"),
        P("expert"),
        P("expert", None, "dp"),
        P("expert", None, "dp"),
        P("expert", "dp", None),
    )
    out_specs = P(("dp", "expert"), None, None)
    return jax.shard_map(body, mesh=mesh, in_specs=in_specs, out_specs=out_specs, check_vma=False)
```

```python
import jax
import jax.numpy as jnp
from jax import lax
from jax.sharding import PartitionSpec as P

CHUNKS = 2


def to_send(kept):
    return kept.astype(jnp.bfloat16)


def added(*terms):
    total = terms[0].astype(jnp.float32)
    for term in terms[1:]:
        total = total + term.astype(jnp.float32)
    return to_send(total)


def spread(value, axis, peers):
    return jnp.stack([value] + [lax.ppermute(value, axis, [(b, a) for a, b in p]) for p in peers])


def fold(value, axis, peers):
    return added(value[0], *[lax.ppermute(value[r + 1], axis, p) for r, p in enumerate(peers)])


def body(
    hidden_states, routes, route_weight, finish_step, group_keep, dest_slot, w_gate, w_up, w_down
):
    expert_count = lax.axis_size("expert")
    replica_count = lax.axis_size("dp")
    row_count, step_count, model_width = hidden_states.shape
    share_rows = row_count // replica_count
    place = dest_slot // (share_rows * expert_count) * share_rows + dest_slot % share_rows
    order = place[None, :] == lax.broadcasted_iota(jnp.int32, (row_count, row_count), 0)
    step_ids = lax.broadcasted_iota(jnp.int32, (row_count, step_count), 1)
    live = (step_ids < finish_step[:, None]) & (group_keep[0] == 1)
    gate_share = route_weight / jnp.sum(route_weight, axis=2, keepdims=True)
    expert_ids = lax.broadcasted_iota(jnp.int32, (1, 1, 1, expert_count), 3)
    picked = (routes[..., None] == expert_ids) & live[:, :, None, None]
    weight = jnp.sum(jnp.where(picked, gate_share[..., None], 0.0), axis=2)
    weight = jnp.sum(jnp.where(order[:, :, None, None], weight[None], 0.0), axis=1)
    my_expert = lax.axis_index("expert")
    my_replica = lax.axis_index("dp")
    all_weight = lax.all_gather(weight, "expert", axis=0, tiled=False)
    mine = lax.broadcasted_iota(jnp.int32, all_weight.shape, 3) == my_expert
    my_weight = jnp.sum(jnp.where(mine, all_weight, 0.0), axis=3)
    ordered = jnp.dot(
        order.astype(jnp.bfloat16),
        hidden_states.reshape(row_count, step_count * model_width),
        preferred_element_type=jnp.float32,
    ).astype(jnp.bfloat16).reshape(row_count, step_count, model_width)
    part = step_count // CHUNKS
    block = share_rows * part
    quad_count = expert_count // 4
    core_peers = [[(e, e ^ 1) for e in range(expert_count)]]
    side_peers = [[(e, e ^ 2) for e in range(expert_count)]]
    quad_peers = [
        [(e, (e + 4 * r) % expert_count) for e in range(expert_count)] for r in range(1, quad_count)
    ]
    dp_peers = [
        [(d, (d + r) % replica_count) for d in range(replica_count)] for r in range(1, replica_count)
    ]
    shape = (2, replica_count, 2, quad_count)
    away = [lax.broadcasted_iota(jnp.int32, shape, k) for k in range(4)]
    owner_expert = (my_expert // 4 + away[3]) % quad_count * 4
    owner_expert += (my_expert // 2 + away[2]) % 2 * 2 + (my_expert + away[0]) % 2
    owner = owner_expert * replica_count + (my_replica + away[1]) % replica_count
    owner = owner.reshape(-1, 1)
    blocks = expert_count * replica_count
    wanted = owner == lax.broadcasted_iota(jnp.int32, (blocks, blocks), 1)
    by_owner = my_weight.reshape(1, blocks, share_rows * step_count)
    my_weight = jnp.sum(jnp.where(wanted[:, :, None], by_owner, 0.0), axis=1)
    my_weight = my_weight.reshape(blocks, share_rows, step_count)
    own = ordered.reshape(replica_count, share_rows, step_count, model_width)
    own = lax.dynamic_index_in_dim(own, my_replica, 0, keepdims=False)
    half = model_width // 2
    results = []
    for c in range(CHUNKS):
        steps = slice(c * part, (c + 1) * part)
        line = spread(own[:, steps].reshape(block, model_width), "expert", quad_peers)
        first = spread(spread(line[..., :half], "expert", side_peers), "dp", dp_peers)
        second = spread(spread(line[..., half:], "dp", dp_peers), "expert", side_peers)
        plane = jnp.concatenate([first, second.swapaxes(0, 1)], axis=-1)
        gathered = spread(plane, "expert", core_peers).reshape(blocks * block, model_width)
        gate_part = jnp.dot(gathered, w_gate[0], preferred_element_type=jnp.float32)
        up_part = jnp.dot(gathered, w_up[0], preferred_element_type=jnp.float32)
        activated = (jax.nn.silu(gate_part) * up_part).astype(jnp.bfloat16)
        expert_result = jnp.dot(activated, w_down[0], preferred_element_type=jnp.float32)
        partial_out = to_send(expert_result * my_weight[:, :, steps].reshape(-1, 1))
        held = partial_out.reshape(shape + (block, model_width))
        held = fold(held, "expert", core_peers)
        first, second = held[..., :half], held[..., half:].swapaxes(0, 1)
        first = fold(first.swapaxes(0, 1), "expert", side_peers)
        second = fold(second.swapaxes(0, 1), "dp", dp_peers)
        first = fold(first, "dp", dp_peers)
        second = fold(second, "expert", side_peers)
        first = fold(first, "expert", quad_peers)
        second = fold(second, "expert", quad_peers)
        summed = jnp.concatenate([first, second], axis=-1)
        results.append(summed.reshape(share_rows, part, model_width))
    return jnp.concatenate(results, axis=1)


def solution(mesh):
    in_specs = (
        P("expert", None, None),
        P("expert", None, None),
        P("expert", None, None),
        P("expert"),
        P("expert"),
        P("expert"),
        P("expert", None, "dp"),
        P("expert", None, "dp"),
        P("expert", "dp", None),
    )
    out_specs = P(("dp", "expert"), None, None)
    return jax.shard_map(body, mesh=mesh, in_specs=in_specs, out_specs=out_specs, check_vma=False)
```
